256 devices in a mesh: seq: 64 (over z, x, core), chan: 4 (over y).
Axes of the slice: x: 4, y: 4, z: 8, core: 2. Of those that a mesh axis runs over, the one named last changes fastest.
Arguments:
- proj_query: float32 [32768, 2048], P('seq', 'chan'), may hold values from -6 to 6
- proj_key: float32 [32768, 2048], P('seq', 'chan'), may hold values from -6 to 6
- proj_value: float32 [32768, 2048], P('seq', 'chan'), may hold values from -6 to 6
- long_filter: float32 [32768, 2048], P('seq', 'chan'), may hold values from -0.03125 to 0.03125
- short_weight: float32 [3, 3, 2048], P(None, None, 'chan'), may hold values from -6.3 to 6.3
- skip_gain: float32 [2048], P('chan'), may hold values from -4 to 4
Outputs:
- mixed: float32 [32768, 2048], P('seq', 'chan')
The draws below stay inside these ranges and needn't reach their ends.
All inputs are finite; a program needn't handle non-finite values.
Results may differ from the reference program's by a relative error of at most 0.00011.
Values sent between devices are 32-bit elements; how exact they have to be, the bound alone decides.
No kernel may reach another device: no remote copies, remote signals or barrier semaphores. Data moves between devices by JAX's collectives and lax.ppermute only.
A program may use at most 64 MiB of HBM per device.

```python
import math
import jax
import jax.numpy as jnp
from jax import lax

TAPS = 3
SEQ = 32768
CH = 2048


def draw_short_weight(key, part):
    key = jax.random.fold_in(key, 7)
    channel = jnp.arange(CH).astype(jnp.float32)
    ramp = 1.0 + 1.7 * channel / CH
    base = jax.random.truncated_normal(key, -4.0, 4.0, (TAPS, 3, CH), jnp.float32) * (1.0 / math.sqrt(3.0))
    return (base * ramp[None, None, :]).astype(jnp.float32)


def level_of(own_key, shape, cuts, low, high):
    def one(axis_at, shards_of):
        steps = jax.random.uniform(jax.random.fold_in(jax.random.fold_in(own_key, 6), axis_at), (shards_of,), jnp.float32, low / len(cuts), high / len(cuts))
        return jnp.repeat(jnp.exp(steps), shape[axis_at] // shards_of).reshape((-1,) + (1,) * (len(shape) - axis_at - 1))

    gain = one(*cuts[0])
    for cut in cuts[1:]:
        gain = gain * one(*cut)
    return gain


def gaussian(key, extent, deviation, most, cuts=(), kind=jnp.bfloat16):
    loudness = level_of(key, extent, cuts, -0.22, 0.18) if cuts else 1.0
    entries = jax.random.normal(key, extent, jnp.float32) * deviation * loudness
    return jnp.minimum(jnp.maximum(entries, -most), most).astype(kind)


def setup_inputs(seed: int = 0) -> dict:
    seeds = jax.random.split(jax.random.key(seed), 7)
    return {
        "proj_query": gaussian(seeds[0], (SEQ, CH), 1.0, 6.0, ((0, 64), (1, 4)), jnp.float32),
        "proj_key": gaussian(seeds[1], (SEQ, CH), 1.0, 6.0, ((0, 64), (1, 4)), jnp.float32),
        "proj_value": gaussian(seeds[2], (SEQ, CH), 1.0, 6.0, ((0, 64), (1, 4)), jnp.float32),
        "long_filter": gaussian(seeds[3], (SEQ, CH), SEQ ** -0.5, 0.03125, ((0, 64), (1, 4)), jnp.float32),
        "short_weight": draw_short_weight(jax.random.fold_in(seeds[6], 71), 0),
        "skip_gain": gaussian(seeds[5], (CH,), 1.0, 4.0, ((0, 4),), jnp.float32),
    }


def short_filter(signal, taps):
    shifted_one = jnp.roll(signal, 1, axis=0)
    shifted_two = jnp.roll(signal, 2, axis=0)
    return taps[0][None, :] * signal + taps[1][None, :] * shifted_one + taps[2][None, :] * shifted_two

def reference(proj_query, proj_key, proj_value, long_filter, short_weight, skip_gain):
    gated_query = short_filter(proj_query, short_weight[:, 0, :])
    gated_key = short_filter(proj_key, short_weight[:, 1, :])
    gated_value = short_filter(proj_value, short_weight[:, 2, :])
    product = gated_key * gated_value
    spectrum = jnp.fft.rfft(product, axis=0) * jnp.fft.rfft(long_filter, axis=0)
    convolved = jnp.fft.irfft(spectrum, n=SEQ, axis=0).astype(product.dtype)
    response = gated_query * (convolved + skip_gain[None, :] * product)
    energy = lax.optimization_barrier(jnp.mean(response * response, axis=1, keepdims=True))
    return response / jnp.sqrt(energy + 1e-06)
```

```python
import functools
import math

import jax
import jax.numpy as jnp
import numpy as np
from jax import lax
from jax.experimental import pallas as pl
from jax.experimental.pallas import tpu as pltpu
from jax.sharding import PartitionSpec as P

LANE = 128
ROWS = 8


def dft8(values, sign):
    def add(a, b):
        if a is None:
            return b
        return a if b is None else a + b

    def sub(a, b):
        if b is None:
            return a
        return -b if a is None else a - b

    def cadd(x, y):
        return (add(x[0], y[0]), add(x[1], y[1]))

    def csub(x, y):
        return (sub(x[0], y[0]), sub(x[1], y[1]))

    def turn(x):
        re, im = x
        if sign > 0:
            return (None if im is None else -im, re)
        return (im, None if re is None else -re)

    def dft4(x):
        a, b = cadd(x[0], x[2]), csub(x[0], x[2])
        c, d = cadd(x[1], x[3]), turn(csub(x[1], x[3]))
        return [cadd(a, c), cadd(b, d), csub(a, c), csub(b, d)]

    even = dft4(values[0::2])
    odd = dft4(values[1::2])
    half = math.sqrt(0.5)
    out = [None] * 8
    for k in range(4):
        re, im = odd[k]
        if k == 0:
            turned = (re, im)
        elif k == 2:
            turned = turn((re, im))
        else:
            first = 1 if k == 1 else -1
            if im is None:
                turned = (first * half * re, sign * half * re)
            else:
                r = re if first > 0 else -re
                i = im if first > 0 else -im
                if sign > 0:
                    turned = (half * (r - im), half * (re + i))
                else:
                    turned = (half * (r + im), half * (i - re))
        out[k] = cadd(even[k], turned)
        out[k + 4] = csub(even[k], turned)
    return out


def cmul(x, y):
    return (x[0] * y[0] - x[1] * y[1], x[0] * y[1] + x[1] * y[0])


CLASSES = (
    [8 * v for v in range(5)]
    + [u + 8 * v for u in (1, 2, 3) for v in range(8)]
    + [4 + 8 * v for v in range(4)]
)
COUNT = len(CLASSES)
SPAN = COUNT * ROWS


def place(k):
    return CLASSES.index(k)


def tables(shards, width):
    total = shards * width
    where = np.arange(width)
    turns = (np.array(CLASSES)[:, None] * where[None, :]) % total
    angle = 2.0 * np.pi * turns / total
    twist = np.stack([np.cos(angle), np.sin(angle)]).astype(np.float32)
    quarter = width // 4
    inner = 2.0 * np.pi * np.arange(4)[:, None] * np.arange(quarter)[None, :] / width
    post = np.stack([np.cos(inner), np.sin(inner)]).astype(np.float32)
    turns = (np.arange(quarter)[:, None] * np.arange(quarter)[None, :]) % quarter
    angle = 2.0 * np.pi * turns / quarter
    c, s = np.cos(angle), np.sin(angle)
    forward = np.block([[c, -s], [s, c]])
    backward = np.block([[c, s], [-s, c]])

    def split(table):
        high = table.astype(np.float32).astype(jnp.bfloat16)
        low = (table - high.astype(np.float64)).astype(np.float32).astype(jnp.bfloat16)
        return np.stack([high, low])

    return twist[:, :, None, :], post[:, :, None, :], split(forward), split(backward)


def split_dot(values, table_ref):
    high = values.astype(jnp.bfloat16)
    low = (values - high.astype(jnp.float32)).astype(jnp.bfloat16)
    t_high, t_low = table_ref[0], table_ref[1]
    dot = functools.partial(jnp.dot, preferred_element_type=jnp.float32)
    return dot(high, t_high) + (dot(low, t_high) + dot(high, t_low))


def sections_forward(x_ref, mid_re, mid_im, stage):
    for lane in range(4):
        sl = slice(lane * LANE, (lane + 1) * LANE)
        for b in range(8):
            col = [(x_ref[8 * a + b, :, sl], None) for a in range(8)]
            out = dft8(col, -1)
            for u in range(5):
                re, im = out[u]
                if u and b:
                    w = (math.cos(2 * math.pi * b * u / 64), -math.sin(2 * math.pi * b * u / 64))
                    if im is None:
                        re, im = re * w[0], re * w[1]
                    else:
                        re, im = cmul((re, im), w)
                stage[0, u * 8 + b] = re
                if im is not None:
                    stage[1, u * 8 + b] = im
        for u in range(5):
            values = []
            for b in range(8):
                real_only = u == 0 or (u == 4 and b == 0)
                values.append(
                    (stage[0, u * 8 + b], None if real_only else stage[1, u * 8 + b])
                )
            out = dft8(values, -1)
            for v in range(8):
                if u + 8 * v in CLASSES:
                    at = place(u + 8 * v)
                    re, im = out[v]
                    mid_re[at, :, sl] = re
                    mid_im[at, :, sl] = jnp.zeros_like(re) if im is None else im


def quarters_forward(mid_re, mid_im, twist, post, spec):
    @pl.loop(0, COUNT)
    def _(at):
        z = []
        for h in range(4):
            sl = slice(h * LANE, (h + 1) * LANE)
            re, im = mid_re[at, :, sl], mid_im[at, :, sl]
            c, s = twist[0, at, :, sl], twist[1, at, :, sl]
            z.append((re * c + im * s, im * c - re * s))
        a = (z[0][0] + z[2][0], z[0][1] + z[2][1])
        b = (z[0][0] - z[2][0], z[0][1] - z[2][1])
        c = (z[1][0] + z[3][0], z[1][1] + z[3][1])
        d = (z[1][1] - z[3][1], z[3][0] - z[1][0])
        outs = [
            (a[0] + c[0], a[1] + c[1]),
            (b[0] + d[0], b[1] + d[1]),
            (a[0] - c[0], a[1] - c[1]),
            (b[0] - d[0], b[1] - d[1]),
        ]
        for q in range(4):
            re, im = outs[q]
            if q:
                c, s = post[0, q], post[1, q]
                re, im = re * c + im * s, im * c - re * s
            rows = pl.ds(pl.multiple_of(q * SPAN + at * ROWS, ROWS), ROWS)
            spec[rows, 0:LANE] = re
            spec[rows, LANE : 2 * LANE] = im


def quarters_backward(spec, mid_re, mid_im, twist, post):
    @pl.loop(0, COUNT)
    def _(at):
        z = []
        for q in range(4):
            rows = pl.ds(pl.multiple_of(q * SPAN + at * ROWS, ROWS), ROWS)
            re, im = spec[rows, 0:LANE], spec[rows, LANE : 2 * LANE]
            if q:
                c, s = post[0, q], post[1, q]
                re, im = re * c - im * s, im * c + re * s
            z.append((re, im))
        a = (z[0][0] + z[2][0], z[0][1] + z[2][1])
        b = (z[0][0] - z[2][0], z[0][1] - z[2][1])
        c = (z[1][0] + z[3][0], z[1][1] + z[3][1])
        d = (z[3][1] - z[1][1], z[1][0] - z[3][0])
        outs = [
            (a[0] + c[0], a[1] + c[1]),
            (b[0] + d[0], b[1] + d[1]),
            (a[0] - c[0], a[1] - c[1]),
            (b[0] - d[0], b[1] - d[1]),
        ]
        for h in range(4):
            sl = slice(h * LANE, (h + 1) * LANE)
            re, im = outs[h]
            c, s = twist[0, at, :, sl], twist[1, at, :, sl]
            mid_re[at, :, sl] = re * c - im * s
            mid_im[at, :, sl] = im * c + re * s


def sections_backward(mid_re, mid_im, y_ref, stage, scale):
    for lane in range(4):
        sl = slice(lane * LANE, (lane + 1) * LANE)
        for u in range(5):
            values = []
            for v in range(8):
                k = u + 8 * v
                if k in CLASSES:
                    at = place(k)
                    if k in (0, 32):
                        values.append((mid_re[at, :, sl], None))
                    else:
                        values.append((mid_re[at, :, sl], mid_im[at, :, sl]))
                elif u == 0:
                    re, im = values[8 - v]
                    values.append((re, -im))
                else:
                    at = place(64 - k)
                    values.append((mid_re[at, :, sl], -mid_im[at, :, sl]))
            out = dft8(values, 1)
            for b in range(8):
                re, im = out[b]
                w = (
                    scale * math.cos(2 * math.pi * b * u / 64),
                    scale * math.sin(2 * math.pi * b * u / 64),
                )
                if u == 0:
                    stage[0, b] = re * w[0]
                elif u == 4:
                    stage[0, 32 + b] = re * w[0] - im * w[1]
                else:
                    if b == 0:
                        re, im = re * w[0], im * w[0]
                    else:
                        re, im = cmul((re, im), w)
                    stage[0, u * 8 + b] = re
                    stage[1, u * 8 + b] = im
        for b in range(8):
            values = [(stage[0, b], None)]
            for u in (1, 2, 3):
                values.append((stage[0, u * 8 + b], stage[1, u * 8 + b]))
            values.append((stage[0, 32 + b], None))
            for u in (3, 2, 1):
                values.append((values[u][0], -values[u][1]))
            out = dft8(values, 1)
            for a in range(8):
                y_ref[8 * a + b, :, sl] = out[a][0]


CHUNK = 176


def spectrum_kernel(x_ref, twist, post, fwd, spec, mid_re, mid_im, stage):
    sections_forward(x_ref, mid_re, mid_im, stage)
    quarters_forward(mid_re, mid_im, twist, post, spec)

    @pl.loop(0, 4 * SPAN // CHUNK)
    def _(i):
        rows = pl.ds(pl.multiple_of(i * CHUNK, CHUNK), CHUNK)
        spec[rows, :] = split_dot(spec[rows, :], fwd)


def convolve_kernel(
    scale, x_ref, filt, twist, post, fwd, bwd, y_ref, mid_re, mid_im, stage, spec
):
    sections_forward(x_ref, mid_re, mid_im, stage)
    quarters_forward(mid_re, mid_im, twist, post, spec)

    @pl.loop(0, 4 * SPAN // CHUNK)
    def _(i):
        rows = pl.ds(pl.multiple_of(i * CHUNK, CHUNK), CHUNK)
        x = split_dot(spec[rows, :], fwd)
        f = filt[rows, :]
        re, im = cmul((x[:, :LANE], x[:, LANE:]), (f[:, :LANE], f[:, LANE:]))
        spec[rows, :] = split_dot(jnp.concatenate([re, im], axis=1), bwd)

    quarters_backward(spec, mid_re, mid_im, twist, post)
    sections_backward(mid_re, mid_im, y_ref, stage, scale)


def fft_scratch(width):
    return [
        pltpu.VMEM((COUNT, ROWS, width), jnp.float32),
        pltpu.VMEM((COUNT, ROWS, width), jnp.float32),
        pltpu.VMEM((2, 40, ROWS, LANE), jnp.float32),
    ]


VM = pl.BlockSpec(memory_space=pltpu.VMEM)
PARAMS = pltpu.CompilerParams(vmem_limit_bytes=40 * 1024 * 1024)


def filter_kernel(first_ref, filter_ref, skip_ref, out_ref):
    height, width = filter_ref.shape
    for p in range(0, height, LANE):
        for c in range(0, width, LANE):
            tile = filter_ref[p : p + LANE, c : c + LANE]
            if p == 0:
                row = lax.broadcasted_iota(jnp.int32, tile.shape, 0)
                direct = skip_ref[:, c : c + LANE] * first_ref[...]
                tile = tile + jnp.where(row == 0, direct, 0.0)
            out_ref[c : c + LANE, p : p + LANE] = tile.T


def short_filter(x_ref, halo, taps, p, c):
    tile = x_ref[p : p + LANE, c : c + LANE]
    if p == 0:
        before = jnp.concatenate([halo, tile[: LANE - 2]], axis=0)
        one = jnp.concatenate([halo[1:2], tile[: LANE - 1]], axis=0)
    else:
        before = x_ref[p - 2 : p + LANE - 2, c : c + LANE]
        one = x_ref[p - 1 : p + LANE - 1, c : c + LANE]
    return taps[0:1] * tile + taps[1:2] * one + taps[2:3] * before


def gate_kernel(key_ref, value_ref, halo_ref, taps_ref, out_ref):
    height, width = key_ref.shape
    for c in range(0, width, LANE):
        sl = slice(c, c + LANE)
        for p in range(0, height, LANE):
            k = short_filter(key_ref, halo_ref[1, :, sl], taps_ref[:, 1, sl], p, c)
            v = short_filter(value_ref, halo_ref[2, :, sl], taps_ref[:, 2, sl], p, c)
            out_ref[sl, p : p + LANE] = (k * v).T


def query_kernel(query_ref, halo_ref, taps_ref, out_ref):
    height, width = query_ref.shape
    for c in range(0, width, LANE):
        sl = slice(c, c + LANE)
        for p in range(0, height, LANE):
            q = short_filter(query_ref, halo_ref[0, :, sl], taps_ref[:, 0, sl], p, c)
            out_ref[sl, p : p + LANE] = q.T


def response_kernel(query_ref, conv_ref, response_ref, energy_ref):
    height, width = query_ref.shape
    total = jnp.zeros((ROWS, width), jnp.float32)
    for r in range(0, height, ROWS):
        value = query_ref[r : r + ROWS, :] * conv_ref[r : r + ROWS, :]
        response_ref[r : r + ROWS, :] = value
        total = total + value * value
    energy_ref[...] = jnp.broadcast_to(jnp.sum(total, axis=0, keepdims=True), energy_ref.shape)


def norm_kernel(channels, response_ref, energy_ref, other_ref, out_ref):
    height, width = response_ref.shape
    mean = (energy_ref[...] + other_ref[...]) / channels
    gain = 1.0 / jnp.sqrt(mean[0:1] + 1e-06)
    for p in range(0, width, LANE):
        for c in range(0, height, LANE):
            tile = response_ref[c : c + LANE, p : p + LANE] * gain[:, p : p + LANE]
            out_ref[p : p + LANE, c : c + LANE] = tile.T


def call(kernel, outs, *args, scratch=(), flops=10_000_000, moved=4_000_000):
    return pl.pallas_call(
        kernel,
        out_shape=outs,
        in_specs=[VM] * len(args),
        out_specs=jax.tree.map(lambda _: VM, outs),
        scratch_shapes=scratch,
        compiler_params=PARAMS,
        cost_estimate=pl.CostEstimate(flops=flops, bytes_accessed=moved, transcendentals=0),
    )(*args)


def exchange(values):
    return lax.all_to_all(values, "seq", split_axis=0, concat_axis=0, tiled=True)


def shifted(value, axis, steps):
    count = lax.axis_size(axis)
    return lax.ppermute(value, axis, [(i, (i + steps) % count) for i in range(count)])


def per_device(proj_query, proj_key, proj_value, long_filter, short_weight, skip_gain):
    height, width = proj_query.shape
    shards = lax.axis_size("seq")
    position = lax.axis_index("seq")
    twist, post, fwd, bwd = (jnp.asarray(t) for t in tables(shards, height))
    block = jax.ShapeDtypeStruct((width, height), jnp.float32)
    cube = jax.ShapeDtypeStruct((shards, ROWS, height), jnp.float32)

    first = jnp.where(position == 0, 1.0, 0.0).astype(jnp.float32)
    first = jnp.broadcast_to(first, (1, LANE))
    filter_t = call(filter_kernel, block, first, long_filter, skip_gain[None, :])
    filter_cols = exchange(filter_t.reshape(shards, ROWS, height))

    tail = jnp.stack([a[height - 2 :, :] for a in (proj_query, proj_key, proj_value)])
    halo = shifted(tail, "seq", 1)
    product_t = call(gate_kernel, block, proj_key, proj_value, halo, short_weight)
    signal_cols = exchange(product_t.reshape(shards, ROWS, height))
    query_t = call(query_kernel, block, proj_query, halo, short_weight)

    spectrum = call(
        spectrum_kernel,
        jax.ShapeDtypeStruct((4 * SPAN, 2 * LANE), jnp.float32),
        filter_cols, twist, post, fwd,
        scratch=fft_scratch(height),
        flops=1_000_000_000,
    )
    conv_cols = call(
        functools.partial(convolve_kernel, 1.0 / (shards * height)),
        cube,
        signal_cols, spectrum, twist, post, fwd, bwd,
        scratch=fft_scratch(height) + [pltpu.VMEM((4 * SPAN, 2 * LANE), jnp.float32)],
        flops=2_000_000_000,
    )
    conv = exchange(conv_cols).reshape(width, height)
    response, energy = call(
        response_kernel,
        (block, jax.ShapeDtypeStruct((ROWS, height), jnp.float32)),
        query_t, conv,
    )
    paired = energy + lax.ppermute(energy, "chan", [(0, 1), (1, 0), (2, 3), (3, 2)])
    other = lax.ppermute(paired, "chan", [(0, 2), (2, 0), (1, 3), (3, 1)])
    channels = width * lax.axis_size("chan")
    return call(
        functools.partial(norm_kernel, float(channels)),
        jax.ShapeDtypeStruct((height, width), jnp.float32),
        response, paired, other,
    )


def solution(mesh):
    return jax.shard_map(
        per_device,
        mesh=mesh,
        in_specs=(
            P("seq", "chan"),
            P("seq", "chan"),
            P("seq", "chan"),
            P("seq", "chan"),
            P(None, None, "chan"),
            P("chan"),
        ),
        out_specs=P("seq", "chan"),
        check_vma=False,
    )
```

```python
import functools
import math

import jax
import jax.numpy as jnp
import numpy as np
from jax import lax
from jax.experimental import pallas as pl
from jax.experimental.pallas import tpu as pltpu
from jax.sharding import PartitionSpec as P

LANE = 128
ROWS = 8


def dft8(values, sign):
    def add(a, b):
        if a is None:
            return b
        return a if b is None else a + b

    def sub(a, b):
        if b is None:
            return a
        return -b if a is None else a - b

    def cadd(x, y):
        return (add(x[0], y[0]), add(x[1], y[1]))

    def csub(x, y):
        return (sub(x[0], y[0]), sub(x[1], y[1]))

    def turn(x):
        re, im = x
        if sign > 0:
            return (None if im is None else -im, re)
        return (im, None if re is None else -re)

    def dft4(x):
        a, b = cadd(x[0], x[2]), csub(x[0], x[2])
        c, d = cadd(x[1], x[3]), turn(csub(x[1], x[3]))
        return [cadd(a, c), cadd(b, d), csub(a, c), csub(b, d)]

    even = dft4(values[0::2])
    odd = dft4(values[1::2])
    half = math.sqrt(0.5)
    out = [None] * 8
    for k in range(4):
        re, im = odd[k]
        if k == 0:
            turned = (re, im)
        elif k == 2:
            turned = turn((re, im))
        else:
            first = 1 if k == 1 else -1
            if im is None:
                turned = (first * half * re, sign * half * re)
            else:
                r = re if first > 0 else -re
                i = im if first > 0 else -im
                if sign > 0:
                    turned = (half * (r - im), half * (re + i))
                else:
                    turned = (half * (r + im), half * (i - re))
        out[k] = cadd(even[k], turned)
        out[k + 4] = csub(even[k], turned)
    return out


def cmul(x, y):
    return (x[0] * y[0] - x[1] * y[1], x[0] * y[1] + x[1] * y[0])


CLASSES = (
    [8 * v for v in range(5)]
    + [u + 8 * v for u in (1, 2, 3) for v in range(8)]
    + [4 + 8 * v for v in range(4)]
)
COUNT = len(CLASSES)
SPAN = COUNT * ROWS


def place(k):
    return CLASSES.index(k)


def tables(shards, width):
    total = shards * width
    where = np.arange(width)
    turns = (np.array(CLASSES)[:, None] * where[None, :]) % total
    angle = 2.0 * np.pi * turns / total
    twist = np.stack([np.cos(angle), np.sin(angle)]).astype(np.float32)
    quarter = width // 4
    inner = 2.0 * np.pi * np.arange(4)[:, None] * np.arange(quarter)[None, :] / width
    post = np.stack([np.cos(inner), np.sin(inner)]).astype(np.float32)
    turns = (np.arange(quarter)[:, None] * np.arange(quarter)[None, :]) % quarter
    angle = 2.0 * np.pi * turns / quarter
    c, s = np.cos(angle), np.sin(angle)
    forward = np.block([[c, -s], [s, c]])
    backward = np.block([[c, s], [-s, c]])

    def split(table):
        high = table.astype(np.float32).astype(jnp.bfloat16)
        low = (table - high.astype(np.float64)).astype(np.float32).astype(jnp.bfloat16)
        return np.stack([high, low])

    return twist[:, :, None, :], post[:, :, None, :], split(forward), split(backward)


def split_dot(values, table_ref):
    high = values.astype(jnp.bfloat16)
    low = (values - high.astype(jnp.float32)).astype(jnp.bfloat16)
    t_high, t_low = table_ref[0], table_ref[1]
    dot = functools.partial(jnp.dot, preferred_element_type=jnp.float32)
    return dot(high, t_high) + (dot(low, t_high) + dot(high, t_low))


UNROLL = 3


def over_classes(body):
    @pl.loop(0, COUNT // UNROLL)
    def _(i):
        for j in range(UNROLL):
            body(i * UNROLL + j)


def sections_forward(x_ref, mid_re, mid_im, stage, lane):
    sl = slice(lane * LANE, (lane + 1) * LANE)
    for b in range(8):
        col = [(x_ref[8 * a + b, :, sl], None) for a in range(8)]
        out = dft8(col, -1)
        for u in range(5):
            re, im = out[u]
            if u and b:
                w = (math.cos(2 * math.pi * b * u / 64), -math.sin(2 * math.pi * b * u / 64))
                if im is None:
                    re, im = re * w[0], re * w[1]
                else:
                    re, im = cmul((re, im), w)
            stage[0, u * 8 + b] = re
            if im is not None:
                stage[1, u * 8 + b] = im
    for u in range(5):
        values = []
        for b in range(8):
            real_only = u == 0 or (u == 4 and b == 0)
            values.append(
                (stage[0, u * 8 + b], None if real_only else stage[1, u * 8 + b])
            )
        out = dft8(values, -1)
        for v in range(8):
            if u + 8 * v in CLASSES:
                at = place(u + 8 * v)
                re, im = out[v]
                mid_re[at, :, sl] = re
                mid_im[at, :, sl] = jnp.zeros_like(re) if im is None else im


def quarters_forward(mid_re, mid_im, twist, post, spec):
    @over_classes
    def _(at):
        z = []
        for h in range(4):
            sl = slice(h * LANE, (h + 1) * LANE)
            re, im = mid_re[at, :, sl], mid_im[at, :, sl]
            c, s = twist[0, at, :, sl], twist[1, at, :, sl]
            z.append((re * c + im * s, im * c - re * s))
        a = (z[0][0] + z[2][0], z[0][1] + z[2][1])
        b = (z[0][0] - z[2][0], z[0][1] - z[2][1])
        c = (z[1][0] + z[3][0], z[1][1] + z[3][1])
        d = (z[1][1] - z[3][1], z[3][0] - z[1][0])
        outs = [
            (a[0] + c[0], a[1] + c[1]),
            (b[0] + d[0], b[1] + d[1]),
            (a[0] - c[0], a[1] - c[1]),
            (b[0] - d[0], b[1] - d[1]),
        ]
        for q in range(4):
            re, im = outs[q]
            if q:
                c, s = post[0, q], post[1, q]
                re, im = re * c + im * s, im * c - re * s
            rows = pl.ds(pl.multiple_of(q * SPAN + at * ROWS, ROWS), ROWS)
            spec[rows, 0:LANE] = re
            spec[rows, LANE : 2 * LANE] = im


def quarters_backward(spec, mid_re, mid_im, twist, post):
    @over_classes
    def _(at):
        z = []
        for q in range(4):
            rows = pl.ds(pl.multiple_of(q * SPAN + at * ROWS, ROWS), ROWS)
            re, im = spec[rows, 0:LANE], spec[rows, LANE : 2 * LANE]
            if q:
                c, s = post[0, q], post[1, q]
                re, im = re * c - im * s, im * c + re * s
            z.append((re, im))
        a = (z[0][0] + z[2][0], z[0][1] + z[2][1])
        b = (z[0][0] - z[2][0], z[0][1] - z[2][1])
        c = (z[1][0] + z[3][0], z[1][1] + z[3][1])
        d = (z[3][1] - z[1][1], z[1][0] - z[3][0])
        outs = [
            (a[0] + c[0], a[1] + c[1]),
            (b[0] + d[0], b[1] + d[1]),
            (a[0] - c[0], a[1] - c[1]),
            (b[0] - d[0], b[1] - d[1]),
        ]
        for h in range(4):
            sl = slice(h * LANE, (h + 1) * LANE)
            re, im = outs[h]
            c, s = twist[0, at, :, sl], twist[1, at, :, sl]
            mid_re[at, :, sl] = re * c - im * s
            mid_im[at, :, sl] = im * c + re * s


def sections_backward(mid_re, mid_im, y_ref, stage, scale, lane):
    sl = slice(lane * LANE, (lane + 1) * LANE)
    for u in range(5):
        values = []
        for v in range(8):
            k = u + 8 * v
            if k in CLASSES:
                at = place(k)
                if k in (0, 32):
                    values.append((mid_re[at, :, sl], None))
                else:
                    values.append((mid_re[at, :, sl], mid_im[at, :, sl]))
            elif u == 0:
                re, im = values[8 - v]
                values.append((re, -im))
            else:
                at = place(64 - k)
                values.append((mid_re[at, :, sl], -mid_im[at, :, sl]))
        out = dft8(values, 1)
        for b in range(8):
            re, im = out[b]
            w = (
                scale * math.cos(2 * math.pi * b * u / 64),
                scale * math.sin(2 * math.pi * b * u / 64),
            )
            if u == 0:
                stage[0, b] = re * w[0]
            elif u == 4:
                stage[0, 32 + b] = re * w[0] - im * w[1]
            else:
                if b == 0:
                    re, im = re * w[0], im * w[0]
                else:
                    re, im = cmul((re, im), w)
                stage[0, u * 8 + b] = re
                stage[1, u * 8 + b] = im
    for b in range(8):
        values = [(stage[0, b], None)]
        for u in (1, 2, 3):
            values.append((stage[0, u * 8 + b], stage[1, u * 8 + b]))
        values.append((stage[0, 32 + b], None))
        for u in (3, 2, 1):
            values.append((values[u][0], -values[u][1]))
        out = dft8(values, 1)
        for a in range(8):
            y_ref[8 * a + b, :, sl] = out[a][0]


def convolve_kernel(
    scale, cols, twist, post, fwd, bwd, out, inbox, y_ref, mid_re, mid_im, stage, filt, spec, got, sent
):
    loads = [
        [
            pltpu.make_async_copy(
                cols.at[:, pl.ds(part * ROWS, ROWS), pl.ds(lane * LANE, LANE)],
                inbox.at[part, :, :, pl.ds(lane * LANE, LANE)],
                got.at[part, lane],
            )
            for lane in range(4)
        ]
        for part in range(2)
    ]
    for part in range(2):
        for copy in loads[part]:
            copy.start()
    for part, into in ((0, filt), (1, spec)):
        for lane in range(4):
            loads[part][lane].wait()
            sections_forward(inbox.at[part], mid_re, mid_im, stage, lane)
        quarters_forward(mid_re, mid_im, twist, post, into)
        if part == 0:
            filt[...] = split_dot(filt[...], fwd)
    x = split_dot(spec[...], fwd)
    f = filt[...]
    re, im = cmul((x[:, :LANE], x[:, LANE:]), (f[:, :LANE], f[:, LANE:]))
    spec[...] = split_dot(jnp.concatenate([re, im], axis=1), bwd)
    quarters_backward(spec, mid_re, mid_im, twist, post)
    stores = []
    for lane in range(4):
        sections_backward(mid_re, mid_im, y_ref, stage, scale, lane)
        sl = pl.ds(lane * LANE, LANE)
        stores.append(pltpu.make_async_copy(y_ref.at[:, :, sl], out.at[:, :, sl], sent.at[lane]))
        stores[-1].start()
    for copy in stores:
        copy.wait()


VM = pl.BlockSpec(memory_space=pltpu.VMEM)
HB = pl.BlockSpec(memory_space=pltpu.HBM)
MIB = 1024 * 1024


def store_columns(out_ref, c, p, at, tile):
    turned = tile.T
    for g in range(tile.shape[1] // ROWS):
        out_ref[c // ROWS + g, at : at + ROWS, p : p + LANE] = turned[g * ROWS : (g + 1) * ROWS]


def short_filter(x_ref, halo, taps, p, c):
    tile = x_ref[p : p + LANE, c : c + LANE]
    if p == 0:
        before = jnp.concatenate([halo, tile[: LANE - 2]], axis=0)
        one = jnp.concatenate([halo[1:2], tile[: LANE - 1]], axis=0)
    else:
        before = x_ref[p - 2 : p + LANE - 2, c : c + LANE]
        one = x_ref[p - 1 : p + LANE - 1, c : c + LANE]
    return taps[0:1] * tile + taps[1:2] * one + taps[2:3] * before


def tail_kernel(query_ref, key_ref, value_ref, out_ref):
    for g, ref in enumerate((query_ref, key_ref, value_ref)):
        out_ref[g] = ref[ROWS - 2 :, :]


def columns_kernel(filter_ref, skip_ref, key_ref, value_ref, taps_ref, out_ref):
    height, width = key_ref.shape
    first = jnp.where(lax.axis_index("seq") == 0, 1.0, 0.0)
    for c in range(0, width, LANE):
        sl = slice(c, c + LANE)
        for p in range(0, height, LANE):
            tile = filter_ref[p : p + LANE, sl]
            if p == 0:
                row = lax.broadcasted_iota(jnp.int32, tile.shape, 0)
                tile = tile + jnp.where(row == 0, skip_ref[:, sl] * first, 0.0)
            store_columns(out_ref, c, p, 0, tile)
            if p:
                k = short_filter(key_ref, None, taps_ref[:, 1, sl], p, c)
                v = short_filter(value_ref, None, taps_ref[:, 2, sl], p, c)
                store_columns(out_ref, c, p, ROWS, k * v)


def edge_kernel(key_ref, value_ref, halo_ref, taps_ref, cols_ref, out_ref):
    del cols_ref
    width = key_ref.shape[1]
    for c in range(0, width, LANE):
        sl = slice(c, c + LANE)
        k = short_filter(key_ref, halo_ref[1, :, sl], taps_ref[:, 1, sl], 0, c)
        v = short_filter(value_ref, halo_ref[2, :, sl], taps_ref[:, 2, sl], 0, c)
        store_columns(out_ref, c, 0, ROWS, k * v)


def query_kernel(query_ref, halo_ref, taps_ref, out_ref):
    height, width = query_ref.shape
    for c in range(0, width, LANE):
        sl = slice(c, c + LANE)
        for p in range(0, height, LANE):
            q = short_filter(query_ref, halo_ref[0, :, sl], taps_ref[:, 0, sl], p, c)
            out_ref[sl, p : p + LANE] = q.T


def response_kernel(query_ref, conv_ref, response_ref, energy_ref):
    height, width = query_ref.shape
    total = jnp.zeros((ROWS, width), jnp.float32)
    for r in range(0, height, ROWS):
        value = query_ref[r : r + ROWS, :] * conv_ref[r : r + ROWS, :]
        response_ref[r : r + ROWS, :] = value
        total = total + value * value
    energy_ref[...] = jnp.broadcast_to(jnp.sum(total, axis=0, keepdims=True), energy_ref.shape)


def norm_kernel(channels, response_ref, energy_ref, e1, e2, e3, out_ref):
    height, width = response_ref.shape
    mean = (energy_ref[...] + e1[...] + e2[...] + e3[...]) / channels
    gain = 1.0 / jnp.sqrt(mean[0:1] + 1e-06)
    for p in range(0, width, LANE):
        for c in range(0, height, LANE):
            tile = response_ref[c : c + LANE, p : p + LANE] * gain[:, p : p + LANE]
            out_ref[p : p + LANE, c : c + LANE] = tile.T


def call(kernel, outs, *args, ins=None, out_specs=None, scratch=(), aliases=None, grid=(),
         vmem=16, flops=10_000_000, moved=4_000_000):
    return pl.pallas_call(
        kernel,
        out_shape=outs,
        grid=grid,
        in_specs=ins or [VM] * len(args),
        out_specs=out_specs or jax.tree.map(lambda _: VM, outs),
        scratch_shapes=scratch,
        input_output_aliases=aliases or {},
        compiler_params=pltpu.CompilerParams(vmem_limit_bytes=vmem * MIB),
        cost_estimate=pl.CostEstimate(flops=flops, bytes_accessed=moved, transcendentals=0),
    )(*args)


def exchange(values):
    return lax.all_to_all(values, "seq", split_axis=0, concat_axis=0, tiled=True)


def shifted(value, axis, steps):
    count = lax.axis_size(axis)
    return lax.ppermute(value, axis, [(i, (i + steps) % count) for i in range(count)])


def per_device(proj_query, proj_key, proj_value, long_filter, short_weight, skip_gain):
    height, width = proj_query.shape
    shards = lax.axis_size("seq")
    twist, post, fwd, bwd = (jnp.asarray(t) for t in tables(shards, height))
    block = jax.ShapeDtypeStruct((width, height), jnp.float32)
    pair = jax.ShapeDtypeStruct((shards, 2 * ROWS, height), jnp.float32)
    cube = jax.ShapeDtypeStruct((shards, ROWS, height), jnp.float32)

    last = pl.BlockSpec((ROWS, width), lambda i: (height // ROWS - 1, 0))
    tail = call(
        tail_kernel,
        jax.ShapeDtypeStruct((3, 2, width), jnp.float32),
        proj_query, proj_key, proj_value,
        grid=(1,),
        ins=[last] * 3,
        out_specs=pl.BlockSpec((3, 2, width), lambda i: (0, 0, 0)),
        moved=100_000,
    )
    halo = shifted(tail, "seq", 1)
    cols = call(
        columns_kernel, pair, long_filter, skip_gain[None, :], proj_key, proj_value, short_weight
    )
    cols = call(
        edge_kernel, pair, proj_key, proj_value, halo, short_weight, cols,
        ins=[VM, VM, VM, VM, VM],
        aliases={4: 0},
        moved=1_000_000,
    )
    cols = exchange(cols)
    query_t = call(query_kernel, block, proj_query, halo, short_weight)

    conv_cols = call(
        functools.partial(convolve_kernel, 1.0 / (shards * height)),
        cube,
        cols, twist, post, fwd, bwd,
        ins=[HB, VM, VM, VM, VM],
        out_specs=HB,
        scratch=[
            pltpu.VMEM((2, shards, ROWS, height), jnp.float32),
            pltpu.VMEM((shards, ROWS, height), jnp.float32),
            pltpu.VMEM((COUNT, ROWS, height), jnp.float32),
            pltpu.VMEM((COUNT, ROWS, height), jnp.float32),
            pltpu.VMEM((2, 40, ROWS, LANE), jnp.float32),
            pltpu.VMEM((4 * SPAN, 2 * LANE), jnp.float32),
            pltpu.VMEM((4 * SPAN, 2 * LANE), jnp.float32),
            pltpu.SemaphoreType.DMA((2, 4)),
            pltpu.SemaphoreType.DMA((4,)),
        ],
        flops=3_000_000_000,
        vmem=32,
    )
    conv = exchange(conv_cols).reshape(width, height)
    response, energy = call(
        response_kernel,
        (block, jax.ShapeDtypeStruct((ROWS, height), jnp.float32)),
        query_t, conv,
    )
    others = [shifted(energy, "chan", k) for k in (2, 1, 3)]
    channels = width * lax.axis_size("chan")
    return call(
        functools.partial(norm_kernel, float(channels)),
        jax.ShapeDtypeStruct((height, width), jnp.float32),
        response, energy, *others,
    )


def solution(mesh):
    return jax.shard_map(
        per_device,
        mesh=mesh,
        in_specs=(
            P("seq", "chan"),
            P("seq", "chan"),
            P("seq", "chan"),
            P("seq", "chan"),
            P(None, None, "chan"),
            P("chan"),
        ),
        out_specs=P("seq", "chan"),
        check_vma=False,
    )
```

```python
import functools
import math

import jax
import jax.numpy as jnp
import numpy as np
from jax import lax
from jax.experimental import pallas as pl
from jax.experimental.pallas import tpu as pltpu
from jax.sharding import PartitionSpec as P

LANE = 128
ROWS = 8


def dft8(values, sign):
    def add(a, b):
        if a is None:
            return b
        return a if b is None else a + b

    def sub(a, b):
        if b is None:
            return a
        return -b if a is None else a - b

    def cadd(x, y):
        return (add(x[0], y[0]), add(x[1], y[1]))

    def csub(x, y):
        return (sub(x[0], y[0]), sub(x[1], y[1]))

    def turn(x):
        re, im = x
        if sign > 0:
            return (None if im is None else -im, re)
        return (im, None if re is None else -re)

    def dft4(x):
        a, b = cadd(x[0], x[2]), csub(x[0], x[2])
        c, d = cadd(x[1], x[3]), turn(csub(x[1], x[3]))
        return [cadd(a, c), cadd(b, d), csub(a, c), csub(b, d)]

    even = dft4(values[0::2])
    odd = dft4(values[1::2])
    half = math.sqrt(0.5)
    out = [None] * 8
    for k in range(4):
        re, im = odd[k]
        if k == 0:
            turned = (re, im)
        elif k == 2:
            turned = turn((re, im))
        else:
            first = 1 if k == 1 else -1
            if im is None:
                turned = (first * half * re, sign * half * re)
            else:
                r = re if first > 0 else -re
                i = im if first > 0 else -im
                if sign > 0:
                    turned = (half * (r - im), half * (re + i))
                else:
                    turned = (half * (r + im), half * (i - re))
        out[k] = cadd(even[k], turned)
        out[k + 4] = csub(even[k], turned)
    return out


def cmul(x, y):
    return (x[0] * y[0] - x[1] * y[1], x[0] * y[1] + x[1] * y[0])


CLASSES = (
    [8 * v for v in range(5)]
    + [u + 8 * v for u in (1, 2, 3) for v in range(8)]
    + [4 + 8 * v for v in range(4)]
)
COUNT = len(CLASSES)
SPAN = COUNT * ROWS


def place(k):
    return CLASSES.index(k)


def tables(shards, width):
    total = shards * width
    where = np.arange(width)
    turns = (np.array(CLASSES)[:, None] * where[None, :]) % total
    angle = 2.0 * np.pi * turns / total
    twist = np.stack([np.cos(angle), np.sin(angle)]).astype(np.float32)
    quarter = width // 4
    inner = 2.0 * np.pi * np.arange(4)[:, None] * np.arange(quarter)[None, :] / width
    post = np.stack([np.cos(inner), np.sin(inner)]).astype(np.float32)
    turns = (np.arange(quarter)[:, None] * np.arange(quarter)[None, :]) % quarter
    angle = 2.0 * np.pi * turns / quarter
    c, s = np.cos(angle), np.sin(angle)
    forward = np.block([[c, -s], [s, c]])
    backward = np.block([[c, s], [-s, c]])

    def split(table):
        high = table.astype(np.float32).astype(jnp.bfloat16)
        low = (table - high.astype(np.float64)).astype(np.float32).astype(jnp.bfloat16)
        return np.concatenate([high, high, low])

    return twist[:, :, None, :], post[:, :, None, :], split(forward), split(backward)


def split_dot(values, table_ref):
    high = values.astype(jnp.bfloat16)
    low = (values - high.astype(jnp.float32)).astype(jnp.bfloat16)
    parts = jnp.concatenate([high, low, high], axis=1)
    return jnp.dot(parts, table_ref[...], preferred_element_type=jnp.float32)


UNROLL = 33


def over_classes(body):
    @pl.loop(0, COUNT // UNROLL)
    def _(i):
        for j in range(UNROLL):
            body(i * UNROLL + j)


def sections_forward(x_ref, at, mid_re, mid_im, stage, lane):
    sl = slice(lane * LANE, (lane + 1) * LANE)
    for b in range(8):
        col = [(x_ref[8 * a + b, at : at + ROWS, sl], None) for a in range(8)]
        out = dft8(col, -1)
        for u in range(5):
            re, im = out[u]
            if u and b:
                w = (math.cos(2 * math.pi * b * u / 64), -math.sin(2 * math.pi * b * u / 64))
                if im is None:
                    re, im = re * w[0], re * w[1]
                else:
                    re, im = cmul((re, im), w)
            stage[0, u * 8 + b] = re
            if im is not None:
                stage[1, u * 8 + b] = im
    for u in range(5):
        values = []
        for b in range(8):
            real_only = u == 0 or (u == 4 and b == 0)
            values.append(
                (stage[0, u * 8 + b], None if real_only else stage[1, u * 8 + b])
            )
        out = dft8(values, -1)
        for v in range(8):
            if u + 8 * v in CLASSES:
                k = place(u + 8 * v)
                re, im = out[v]
                mid_re[k, :, sl] = re
                mid_im[k, :, sl] = jnp.zeros_like(re) if im is None else im


def quarters_forward(mid_re, mid_im, twist, post, spec):
    @over_classes
    def _(at):
        z = []
        for h in range(4):
            sl = slice(h * LANE, (h + 1) * LANE)
            re, im = mid_re[at, :, sl], mid_im[at, :, sl]
            c, s = twist[0, at, :, sl], twist[1, at, :, sl]
            z.append((re * c + im * s, im * c - re * s))
        a = (z[0][0] + z[2][0], z[0][1] + z[2][1])
        b = (z[0][0] - z[2][0], z[0][1] - z[2][1])
        c = (z[1][0] + z[3][0], z[1][1] + z[3][1])
        d = (z[1][1] - z[3][1], z[3][0] - z[1][0])
        outs = [
            (a[0] + c[0], a[1] + c[1]),
            (b[0] + d[0], b[1] + d[1]),
            (a[0] - c[0], a[1] - c[1]),
            (b[0] - d[0], b[1] - d[1]),
        ]
        for q in range(4):
            re, im = outs[q]
            if q:
                c, s = post[0, q], post[1, q]
                re, im = re * c + im * s, im * c - re * s
            rows = pl.ds(pl.multiple_of(q * SPAN + at * ROWS, ROWS), ROWS)
            spec[rows, 0:LANE] = re
            spec[rows, LANE : 2 * LANE] = im


def quarters_backward(spec, mid_re, mid_im, twist, post):
    @over_classes
    def _(at):
        z = []
        for q in range(4):
            rows = pl.ds(pl.multiple_of(q * SPAN + at * ROWS, ROWS), ROWS)
            re, im = spec[rows, 0:LANE], spec[rows, LANE : 2 * LANE]
            if q:
                c, s = post[0, q], post[1, q]
                re, im = re * c - im * s, im * c + re * s
            z.append((re, im))
        a = (z[0][0] + z[2][0], z[0][1] + z[2][1])
        b = (z[0][0] - z[2][0], z[0][1] - z[2][1])
        c = (z[1][0] + z[3][0], z[1][1] + z[3][1])
        d = (z[3][1] - z[1][1], z[1][0] - z[3][0])
        outs = [
            (a[0] + c[0], a[1] + c[1]),
            (b[0] + d[0], b[1] + d[1]),
            (a[0] - c[0], a[1] - c[1]),
            (b[0] - d[0], b[1] - d[1]),
        ]
        for h in range(4):
            sl = slice(h * LANE, (h + 1) * LANE)
            re, im = outs[h]
            c, s = twist[0, at, :, sl], twist[1, at, :, sl]
            mid_re[at, :, sl] = re * c - im * s
            mid_im[at, :, sl] = im * c + re * s


def sections_backward(mid_re, mid_im, y_ref, stage, scale, lane):
    sl = slice(lane * LANE, (lane + 1) * LANE)
    for u in range(5):
        values = []
        for v in range(8):
            k = u + 8 * v
            if k in CLASSES:
                at = place(k)
                if k in (0, 32):
                    values.append((mid_re[at, :, sl], None))
                else:
                    values.append((mid_re[at, :, sl], mid_im[at, :, sl]))
            elif u == 0:
                re, im = values[8 - v]
                values.append((re, -im))
            else:
                at = place(64 - k)
                values.append((mid_re[at, :, sl], -mid_im[at, :, sl]))
        out = dft8(values, 1)
        for b in range(8):
            re, im = out[b]
            w = (
                scale * math.cos(2 * math.pi * b * u / 64),
                scale * math.sin(2 * math.pi * b * u / 64),
            )
            if u == 0:
                stage[0, b] = re * w[0]
            elif u == 4:
                stage[0, 32 + b] = re * w[0] - im * w[1]
            else:
                if b == 0:
                    re, im = re * w[0], im * w[0]
                else:
                    re, im = cmul((re, im), w)
                stage[0, u * 8 + b] = re
                stage[1, u * 8 + b] = im
    for b in range(8):
        values = [(stage[0, b], None)]
        for u in (1, 2, 3):
            values.append((stage[0, u * 8 + b], stage[1, u * 8 + b]))
        values.append((stage[0, 32 + b], None))
        for u in (3, 2, 1):
            values.append((values[u][0], -values[u][1]))
        out = dft8(values, 1)
        for a in range(8):
            y_ref[8 * a + b, :, sl] = out[a][0]


def convolve_kernel(
    scale, cols, twist, post, fwd, bwd, y_ref, mid_re, mid_im, stage, filt, spec
):
    for part, into in ((0, filt), (1, spec)):
        for lane in range(4):
            sections_forward(cols, part * ROWS, mid_re, mid_im, stage, lane)
        quarters_forward(mid_re, mid_im, twist, post, into)
        if part == 0:
            filt[...] = split_dot(filt[...], fwd)
    x = split_dot(spec[...], fwd)
    f = filt[...]
    re, im = cmul((x[:, :LANE], x[:, LANE:]), (f[:, :LANE], f[:, LANE:]))
    spec[...] = split_dot(jnp.concatenate([re, im], axis=1), bwd)
    quarters_backward(spec, mid_re, mid_im, twist, post)
    for lane in range(4):
        sections_backward(mid_re, mid_im, y_ref, stage, scale, lane)


VM = pl.BlockSpec(memory_space=pltpu.VMEM)
HB = pl.BlockSpec(memory_space=pltpu.HBM)
MIB = 1024 * 1024


def store_columns(out_ref, c, p, at, tile):
    turned = tile.T
    for g in range(tile.shape[1] // ROWS):
        out_ref[c // ROWS + g, at : at + ROWS, p : p + LANE] = turned[g * ROWS : (g + 1) * ROWS]


def short_filter(x_ref, halo, taps, p, c):
    tile = x_ref[p : p + LANE, c : c + LANE]
    if p == 0:
        before = jnp.concatenate([halo, tile[: LANE - 2]], axis=0)
        one = jnp.concatenate([halo[1:2], tile[: LANE - 1]], axis=0)
    else:
        before = x_ref[p - 2 : p + LANE - 2, c : c + LANE]
        one = x_ref[p - 1 : p + LANE - 1, c : c + LANE]
    return taps[0:1] * tile + taps[1:2] * one + taps[2:3] * before


def tail_kernel(query_ref, key_ref, value_ref, out_ref):
    for g, ref in enumerate((query_ref, key_ref, value_ref)):
        out_ref[g] = ref[ROWS - 2 :, :]


def columns_kernel(filter_ref, key_ref, value_ref, taps_ref, out_ref):
    height, width = key_ref.shape
    first = jnp.where(lax.axis_index("seq") == 0, 1.0, 0.0)
    for c in range(0, width, LANE):
        sl = slice(c, c + LANE)
        for p in range(0, height, LANE):
            tile = filter_ref[p : p + LANE, sl]
            if p == 0:
                row = lax.broadcasted_iota(jnp.int32, tile.shape, 0)
                tile = tile + jnp.where(row == 0, taps_ref[3, 0:1, sl] * first, 0.0)
            store_columns(out_ref, c, p, 0, tile)
            if p:
                k = short_filter(key_ref, None, taps_ref[:, 1, sl], p, c)
                v = short_filter(value_ref, None, taps_ref[:, 2, sl], p, c)
                store_columns(out_ref, c, p, ROWS, k * v)


def edge_kernel(key_ref, value_ref, halo_ref, taps_ref, cols_ref, out_ref):
    del cols_ref
    width = key_ref.shape[1]
    for c in range(0, width, LANE):
        sl = slice(c, c + LANE)
        k = short_filter(key_ref, halo_ref[1, :, sl], taps_ref[:, 1, sl], 0, c)
        v = short_filter(value_ref, halo_ref[2, :, sl], taps_ref[:, 2, sl], 0, c)
        store_columns(out_ref, c, 0, ROWS, k * v)


def query_kernel(query_ref, halo_ref, taps_ref, out_ref):
    height, width = query_ref.shape
    for c in range(0, width, LANE):
        sl = slice(c, c + LANE)
        for p in range(0, height, LANE):
            q = short_filter(query_ref, halo_ref[0, :, sl], taps_ref[:, 0, sl], p, c)
            out_ref[sl, p : p + LANE] = q.T


def response_kernel(query_ref, conv_ref, response_ref, energy_ref):
    height, width = query_ref.shape
    total = jnp.zeros((ROWS, width), jnp.float32)
    for r in range(0, height, ROWS):
        value = query_ref[r : r + ROWS, :] * conv_ref[r : r + ROWS, :]
        response_ref[r : r + ROWS, :] = value
        total = total + value * value
    energy_ref[...] = jnp.broadcast_to(jnp.sum(total, axis=0, keepdims=True), energy_ref.shape)


def norm_kernel(channels, response_ref, energy_ref, e1, e2, e3, out_ref, box, sems):
    height, width = response_ref.shape
    mean = (energy_ref[...] + e1[...] + e2[...] + e3[...]) / channels
    gain = 1.0 / jnp.sqrt(mean[0:1] + 1e-06)
    copies = []
    for i, p in enumerate(range(0, width, LANE)):
        for c in range(0, height, LANE):
            tile = response_ref[c : c + LANE, p : p + LANE] * gain[:, p : p + LANE]
            box[p : p + LANE, c : c + LANE] = tile.T
        rows = pl.ds(p, LANE)
        copies.append(pltpu.make_async_copy(box.at[rows], out_ref.at[rows], sems.at[i]))
        copies[-1].start()
    for copy in copies:
        copy.wait()


def call(kernel, outs, *args, ins=None, out_specs=None, scratch=(), aliases=None, grid=(),
         vmem=16, flops=10_000_000, moved=4_000_000):
    return pl.pallas_call(
        kernel,
        out_shape=outs,
        grid=grid,
        in_specs=ins or [VM] * len(args),
        out_specs=out_specs or jax.tree.map(lambda _: VM, outs),
        scratch_shapes=scratch,
        input_output_aliases=aliases or {},
        compiler_params=pltpu.CompilerParams(vmem_limit_bytes=vmem * MIB),
        cost_estimate=pl.CostEstimate(flops=flops, bytes_accessed=moved, transcendentals=0),
    )(*args)


def exchange(values):
    return lax.all_to_all(values, "seq", split_axis=0, concat_axis=0, tiled=True)


def shifted(value, axis, steps):
    count = lax.axis_size(axis)
    return lax.ppermute(value, axis, [(i, (i + steps) % count) for i in range(count)])


def per_device(proj_query, proj_key, proj_value, long_filter, short_weight, skip_gain):
    height, width = proj_query.shape
    shards = lax.axis_size("seq")
    twist, post, fwd, bwd = (jnp.asarray(t) for t in tables(shards, height))
    block = jax.ShapeDtypeStruct((width, height), jnp.float32)
    pair = jax.ShapeDtypeStruct((shards, 2 * ROWS, height), jnp.float32)
    cube = jax.ShapeDtypeStruct((shards, ROWS, height), jnp.float32)

    direct = jnp.broadcast_to(skip_gain, (1, 3, width))
    taps = jnp.concatenate([short_weight, direct])
    last = pl.BlockSpec((ROWS, width), lambda i: (height // ROWS - 1, 0))
    tail = call(
        tail_kernel,
        jax.ShapeDtypeStruct((3, 2, width), jnp.float32),
        proj_query[height - ROWS :, :], proj_key, proj_value,
        grid=(1,),
        ins=[pl.BlockSpec((ROWS, width), lambda i: (0, 0)), last, last],
        out_specs=pl.BlockSpec((3, 2, width), lambda i: (0, 0, 0)),
        moved=100_000,
    )
    halo = shifted(tail, "seq", 1)
    cols = call(
        columns_kernel, pair, long_filter, proj_key, proj_value, taps
    )
    cols = call(
        edge_kernel, pair, proj_key, proj_value, halo, taps, cols,
        aliases={4: 0},
        moved=1_000_000,
    )
    cols = exchange(cols)
    query_t = call(query_kernel, block, proj_query, halo, taps)

    conv_cols = call(
        functools.partial(convolve_kernel, 1.0 / (shards * height)),
        cube,
        cols, twist, post, fwd, bwd,
        scratch=[
            pltpu.VMEM((COUNT, ROWS, height), jnp.float32),
            pltpu.VMEM((COUNT, ROWS, height), jnp.float32),
            pltpu.VMEM((2, 40, ROWS, LANE), jnp.float32),
            pltpu.VMEM((4 * SPAN, 2 * LANE), jnp.float32),
            pltpu.VMEM((4 * SPAN, 2 * LANE), jnp.float32),
        ],
        flops=3_000_000_000,
        vmem=24,
    )
    conv = exchange(conv_cols).reshape(width, height)
    response, energy = call(
        response_kernel,
        (block, jax.ShapeDtypeStruct((ROWS, height), jnp.float32)),
        query_t, conv,
    )
    others = [shifted(energy, "chan", k) for k in (2, 1, 3)]
    channels = width * lax.axis_size("chan")
    return call(
        functools.partial(norm_kernel, float(channels)),
        jax.ShapeDtypeStruct((height, width), jnp.float32),
        response, energy, *others,
        out_specs=HB,
        scratch=[
            pltpu.VMEM((height, width), jnp.float32),
            pltpu.SemaphoreType.DMA((height // LANE,)),
        ],
    )


def solution(mesh):
    return jax.shard_map(
        per_device,
        mesh=mesh,
        in_specs=(
            P("seq", "chan"),
            P("seq", "chan"),
            P("seq", "chan"),
            P("seq", "chan"),
            P(None, None, "chan"),
            P("chan"),
        ),
        out_specs=P("seq", "chan"),
        check_vma=False,
    )
```

```python
import functools
import math

import jax
import jax.numpy as jnp
import numpy as np
from jax import lax
from jax.experimental import pallas as pl
from jax.experimental.pallas import tpu as pltpu
from jax.sharding import PartitionSpec as P

LANE = 128
ROWS = 8


def dft8(values, sign):
    def add(a, b):
        if a is None:
            return b
        return a if b is None else a + b

    def sub(a, b):
        if b is None:
            return a
        return -b if a is None else a - b

    def cadd(x, y):
        return (add(x[0], y[0]), add(x[1], y[1]))

    def csub(x, y):
        return (sub(x[0], y[0]), sub(x[1], y[1]))

    def turn(x):
        re, im = x
        if sign > 0:
            return (None if im is None else -im, re)
        return (im, None if re is None else -re)

    def dft4(x):
        a, b = cadd(x[0], x[2]), csub(x[0], x[2])
        c, d = cadd(x[1], x[3]), turn(csub(x[1], x[3]))
        return [cadd(a, c), cadd(b, d), csub(a, c), csub(b, d)]

    even = dft4(values[0::2])
    odd = dft4(values[1::2])
    half = math.sqrt(0.5)
    out = [None] * 8
    for k in range(4):
        re, im = odd[k]
        if k == 0:
            turned = (re, im)
        elif k == 2:
            turned = turn((re, im))
        else:
            first = 1 if k == 1 else -1
            if im is None:
                turned = (first * half * re, sign * half * re)
            else:
                r = re if first > 0 else -re
                i = im if first > 0 else -im
                if sign > 0:
                    turned = (half * (r - im), half * (re + i))
                else:
                    turned = (half * (r + im), half * (i - re))
        out[k] = cadd(even[k], turned)
        out[k + 4] = csub(even[k], turned)
    return out


def cmul(x, y):
    return (x[0] * y[0] - x[1] * y[1], x[0] * y[1] + x[1] * y[0])


CLASSES = (
    [8 * v for v in range(5)]
    + [u + 8 * v for u in (1, 2, 3) for v in range(8)]
    + [4 + 8 * v for v in range(4)]
)
COUNT = len(CLASSES)
SPAN = COUNT * ROWS


def place(k):
    return CLASSES.index(k)


def tables(shards, width):
    total = shards * width
    where = np.arange(width)
    turns = (np.array(CLASSES)[:, None] * where[None, :]) % total
    angle = 2.0 * np.pi * turns / total
    twist = np.stack([np.cos(angle), np.sin(angle)]).astype(np.float32)
    quarter = width // 4
    inner = 2.0 * np.pi * np.arange(4)[:, None] * np.arange(quarter)[None, :] / width
    post = np.stack([np.cos(inner), np.sin(inner)]).astype(np.float32)
    turns = (np.arange(quarter)[:, None] * np.arange(quarter)[None, :]) % quarter
    angle = 2.0 * np.pi * turns / quarter
    c, s = np.cos(angle), np.sin(angle)
    forward = np.block([[c, -s], [s, c]])
    backward = np.block([[c, s], [-s, c]])

    def split(table):
        high = table.astype(np.float32).astype(jnp.bfloat16)
        low = (table - high.astype(np.float64)).astype(np.float32).astype(jnp.bfloat16)
        return np.concatenate([high, high, low])

    return twist[:, :, None, :], post[:, :, None, :], split(forward), split(backward)


def split_dot(values, table_ref):
    high = values.astype(jnp.bfloat16)
    low = (values - high.astype(jnp.float32)).astype(jnp.bfloat16)
    parts = jnp.concatenate([high, low, high], axis=1)
    return jnp.dot(parts, table_ref[...], preferred_element_type=jnp.float32)


UNROLL = 33


def over_classes(body):
    @pl.loop(0, COUNT // UNROLL)
    def _(i):
        for j in range(UNROLL):
            body(i * UNROLL + j)


def sections_forward(x_ref, at, mid_re, mid_im, stage, lane):
    sl = slice(lane * LANE, (lane + 1) * LANE)
    for b in range(8):
        col = [(x_ref[8 * a + b, at : at + ROWS, sl], None) for a in range(8)]
        out = dft8(col, -1)
        for u in range(5):
            re, im = out[u]
            if u and b:
                w = (math.cos(2 * math.pi * b * u / 64), -math.sin(2 * math.pi * b * u / 64))
                if im is None:
                    re, im = re * w[0], re * w[1]
                else:
                    re, im = cmul((re, im), w)
            stage[0, u * 8 + b] = re
            if im is not None:
                stage[1, u * 8 + b] = im
    for u in range(5):
        values = []
        for b in range(8):
            real_only = u == 0 or (u == 4 and b == 0)
            values.append(
                (stage[0, u * 8 + b], None if real_only else stage[1, u * 8 + b])
            )
        out = dft8(values, -1)
        for v in range(8):
            if u + 8 * v in CLASSES:
                k = place(u + 8 * v)
                re, im = out[v]
                mid_re[k, :, sl] = re
                mid_im[k, :, sl] = jnp.zeros_like(re) if im is None else im


def quarters_forward(mid_re, mid_im, twist, post, spec):
    @over_classes
    def _(at):
        z = []
        for h in range(4):
            sl = slice(h * LANE, (h + 1) * LANE)
            re, im = mid_re[at, :, sl], mid_im[at, :, sl]
            c, s = twist[0, at, :, sl], twist[1, at, :, sl]
            z.append((re * c + im * s, im * c - re * s))
        a = (z[0][0] + z[2][0], z[0][1] + z[2][1])
        b = (z[0][0] - z[2][0], z[0][1] - z[2][1])
        c = (z[1][0] + z[3][0], z[1][1] + z[3][1])
        d = (z[1][1] - z[3][1], z[3][0] - z[1][0])
        outs = [
            (a[0] + c[0], a[1] + c[1]),
            (b[0] + d[0], b[1] + d[1]),
            (a[0] - c[0], a[1] - c[1]),
            (b[0] - d[0], b[1] - d[1]),
        ]
        for q in range(4):
            re, im = outs[q]
            if q:
                c, s = post[0, q], post[1, q]
                re, im = re * c + im * s, im * c - re * s
            rows = pl.ds(pl.multiple_of(q * SPAN + at * ROWS, ROWS), ROWS)
            spec[rows, 0:LANE] = re
            spec[rows, LANE : 2 * LANE] = im


def quarters_backward(spec, mid_re, mid_im, twist, post):
    @over_classes
    def _(at):
        z = []
        for q in range(4):
            rows = pl.ds(pl.multiple_of(q * SPAN + at * ROWS, ROWS), ROWS)
            re, im = spec[rows, 0:LANE], spec[rows, LANE : 2 * LANE]
            if q:
                c, s = post[0, q], post[1, q]
                re, im = re * c - im * s, im * c + re * s
            z.append((re, im))
        a = (z[0][0] + z[2][0], z[0][1] + z[2][1])
        b = (z[0][0] - z[2][0], z[0][1] - z[2][1])
        c = (z[1][0] + z[3][0], z[1][1] + z[3][1])
        d = (z[3][1] - z[1][1], z[1][0] - z[3][0])
        outs = [
            (a[0] + c[0], a[1] + c[1]),
            (b[0] + d[0], b[1] + d[1]),
            (a[0] - c[0], a[1] - c[1]),
            (b[0] - d[0], b[1] - d[1]),
        ]
        for h in range(4):
            sl = slice(h * LANE, (h + 1) * LANE)
            re, im = outs[h]
            c, s = twist[0, at, :, sl], twist[1, at, :, sl]
            mid_re[at, :, sl] = re * c - im * s
            mid_im[at, :, sl] = im * c + re * s


def sections_backward(mid_re, mid_im, y_ref, stage, scale, lane):
    sl = slice(lane * LANE, (lane + 1) * LANE)
    for u in range(5):
        values = []
        for v in range(8):
            k = u + 8 * v
            if k in CLASSES:
                at = place(k)
                if k in (0, 32):
                    values.append((mid_re[at, :, sl], None))
                else:
                    values.append((mid_re[at, :, sl], mid_im[at, :, sl]))
            elif u == 0:
                re, im = values[8 - v]
                values.append((re, -im))
            else:
                at = place(64 - k)
                values.append((mid_re[at, :, sl], -mid_im[at, :, sl]))
        out = dft8(values, 1)
        for b in range(8):
            re, im = out[b]
            w = (
                scale * math.cos(2 * math.pi * b * u / 64),
                scale * math.sin(2 * math.pi * b * u / 64),
            )
            if u == 0:
                stage[0, b] = re * w[0]
            elif u == 4:
                stage[0, 32 + b] = re * w[0] - im * w[1]
            else:
                if b == 0:
                    re, im = re * w[0], im * w[0]
                else:
                    re, im = cmul((re, im), w)
                stage[0, u * 8 + b] = re
                stage[1, u * 8 + b] = im
    for b in range(8):
        values = [(stage[0, b], None)]
        for u in (1, 2, 3):
            values.append((stage[0, u * 8 + b], stage[1, u * 8 + b]))
        values.append((stage[0, 32 + b], None))
        for u in (3, 2, 1):
            values.append((values[u][0], -values[u][1]))
        out = dft8(values, 1)
        for a in range(8):
            y_ref[8 * a + b, :, sl] = out[a][0]


def convolve_kernel(
    scale, cols, twist, post, fwd, bwd, y_ref, mid_re, mid_im, stage, filt, spec
):
    for part, into in ((0, filt), (1, spec)):
        for lane in range(4):
            sections_forward(cols, part * ROWS, mid_re, mid_im, stage, lane)
        quarters_forward(mid_re, mid_im, twist, post, into)
        if part == 0:
            filt[...] = split_dot(filt[...], fwd)
    x = split_dot(spec[...], fwd)
    f = filt[...]
    re, im = cmul((x[:, :LANE], x[:, LANE:]), (f[:, :LANE], f[:, LANE:]))
    spec[...] = split_dot(jnp.concatenate([re, im], axis=1), bwd)
    quarters_backward(spec, mid_re, mid_im, twist, post)
    for lane in range(4):
        sections_backward(mid_re, mid_im, y_ref, stage, scale, lane)


VM = pl.BlockSpec(memory_space=pltpu.VMEM)
HB = pl.BlockSpec(memory_space=pltpu.HBM)
MIB = 1024 * 1024


def store_columns(out_ref, c, p, at, tile):
    turned = tile.T
    for g in range(tile.shape[1] // ROWS):
        out_ref[c // ROWS + g, at : at + ROWS, p : p + LANE] = turned[g * ROWS : (g + 1) * ROWS]


def short_filter(x_ref, halo, taps, p, c):
    tile = x_ref[p : p + LANE, c : c + LANE]
    if p == 0:
        before = jnp.concatenate([halo, tile[: LANE - 2]], axis=0)
        one = jnp.concatenate([halo[1:2], tile[: LANE - 1]], axis=0)
    else:
        before = x_ref[p - 2 : p + LANE - 2, c : c + LANE]
        one = x_ref[p - 1 : p + LANE - 1, c : c + LANE]
    return taps[0] * tile + taps[1] * one + taps[2] * before


def small_kernel(query_ref, key_ref, value_ref, taps_ref, skip_ref, out_ref, box, taps, skip, sems):
    height = query_ref.shape[0]
    copies = [
        pltpu.make_async_copy(ref.at[pl.ds(height - ROWS, ROWS)], box.at[g], sems.at[g])
        for g, ref in enumerate((query_ref, key_ref, value_ref))
    ]
    copies.append(pltpu.make_async_copy(taps_ref, taps, sems.at[3]))
    copies.append(pltpu.make_async_copy(skip_ref, skip, sems.at[4]))
    for copy in copies:
        copy.start()
    for copy in copies:
        copy.wait()
    for g in range(3):
        out_ref[2 * g : 2 * g + 2, :] = box[g, ROWS - 2 :, :]
        out_ref[6 + 3 * g : 9 + 3 * g, :] = taps[g]
    out_ref[15:16, :] = skip[...]


def taps_of(small_ref, g, sl):
    return [small_ref[6 + 3 * i + g : 7 + 3 * i + g, sl] for i in range(3)]


def columns_kernel(filter_ref, key_ref, value_ref, small_ref, out_ref):
    height, width = key_ref.shape
    first = jnp.where(lax.axis_index("seq") == 0, 1.0, 0.0)
    for c in range(0, width, LANE):
        sl = slice(c, c + LANE)
        for p in range(0, height, LANE):
            tile = filter_ref[p : p + LANE, sl]
            if p == 0:
                row = lax.broadcasted_iota(jnp.int32, tile.shape, 0)
                tile = tile + jnp.where(row == 0, small_ref[15:16, sl] * first, 0.0)
            store_columns(out_ref, c, p, 0, tile)
            if p:
                k = short_filter(key_ref, None, taps_of(small_ref, 1, sl), p, c)
                v = short_filter(value_ref, None, taps_of(small_ref, 2, sl), p, c)
                store_columns(out_ref, c, p, ROWS, k * v)


def edge_kernel(key_ref, value_ref, halo_ref, small_ref, cols_ref, out_ref):
    del cols_ref
    width = key_ref.shape[1]
    for c in range(0, width, LANE):
        sl = slice(c, c + LANE)
        k = short_filter(key_ref, halo_ref[2 : 4, sl], taps_of(small_ref, 1, sl), 0, c)
        v = short_filter(value_ref, halo_ref[4 : 6, sl], taps_of(small_ref, 2, sl), 0, c)
        store_columns(out_ref, c, 0, ROWS, k * v)


def query_kernel(query_ref, halo_ref, small_ref, out_ref):
    height, width = query_ref.shape
    for c in range(0, width, LANE):
        sl = slice(c, c + LANE)
        for p in range(0, height, LANE):
            q = short_filter(query_ref, halo_ref[0 : 2, sl], taps_of(small_ref, 0, sl), p, c)
            out_ref[sl, p : p + LANE] = q.T


def response_kernel(query_ref, conv_ref, response_ref, energy_ref):
    height, width = query_ref.shape
    total = jnp.zeros((ROWS, width), jnp.float32)
    for r in range(0, height, ROWS):
        value = query_ref[r : r + ROWS, :] * conv_ref[r : r + ROWS, :]
        response_ref[r : r + ROWS, :] = value
        total = total + value * value
    energy_ref[...] = jnp.broadcast_to(jnp.sum(total, axis=0, keepdims=True), energy_ref.shape)


def norm_kernel(channels, response_ref, energy_ref, e1, e2, e3, out_ref, box, sems):
    height, width = response_ref.shape
    mean = (energy_ref[...] + e1[...] + e2[...] + e3[...]) / channels
    gain = 1.0 / jnp.sqrt(mean[0:1] + 1e-06)
    copies = []
    for i, p in enumerate(range(0, width, LANE)):
        for c in range(0, height, LANE):
            tile = response_ref[c : c + LANE, p : p + LANE] * gain[:, p : p + LANE]
            box[p : p + LANE, c : c + LANE] = tile.T
        rows = pl.ds(p, LANE)
        copies.append(pltpu.make_async_copy(box.at[rows], out_ref.at[rows], sems.at[i]))
        copies[-1].start()
    for copy in copies:
        copy.wait()


def call(kernel, outs, *args, ins=None, out_specs=None, scratch=(), aliases=None, grid=(),
         vmem=16, flops=10_000_000, moved=4_000_000):
    return pl.pallas_call(
        kernel,
        out_shape=outs,
        grid=grid,
        in_specs=ins or [VM] * len(args),
        out_specs=out_specs or jax.tree.map(lambda _: VM, outs),
        scratch_shapes=scratch,
        input_output_aliases=aliases or {},
        compiler_params=pltpu.CompilerParams(vmem_limit_bytes=vmem * MIB),
        cost_estimate=pl.CostEstimate(flops=flops, bytes_accessed=moved, transcendentals=0),
    )(*args)


def exchange(values):
    return lax.all_to_all(values, "seq", split_axis=0, concat_axis=0, tiled=True)


def shifted(value, axis, steps):
    count = lax.axis_size(axis)
    return lax.ppermute(value, axis, [(i, (i + steps) % count) for i in range(count)])


def per_device(proj_query, proj_key, proj_value, long_filter, short_weight, skip_gain):
    height, width = proj_query.shape
    shards = lax.axis_size("seq")
    twist, post, fwd, bwd = (jnp.asarray(t) for t in tables(shards, height))
    block = jax.ShapeDtypeStruct((width, height), jnp.float32)
    pair = jax.ShapeDtypeStruct((shards, 2 * ROWS, height), jnp.float32)
    cube = jax.ShapeDtypeStruct((shards, ROWS, height), jnp.float32)

    small = call(
        small_kernel,
        jax.ShapeDtypeStruct((2 * ROWS, width), jnp.float32),
        proj_query, proj_key, proj_value, short_weight, skip_gain[None, :],
        ins=[HB] * 5,
        scratch=[
            pltpu.VMEM((3, ROWS, width), jnp.float32),
            pltpu.VMEM((3, 3, width), jnp.float32),
            pltpu.VMEM((1, width), jnp.float32),
            pltpu.SemaphoreType.DMA((5,)),
        ],
        moved=100_000,
        vmem=60,
    )
    halo = shifted(small, "seq", 1)
    cols = call(
        columns_kernel, pair, long_filter, proj_key, proj_value, small
    )
    cols = call(
        edge_kernel, pair, proj_key, proj_value, halo, small, cols,
        aliases={4: 0},
        moved=1_000_000,
    )
    cols = exchange(cols)
    query_t = call(query_kernel, block, proj_query, halo, small)

    conv_cols = call(
        functools.partial(convolve_kernel, 1.0 / (shards * height)),
        cube,
        cols, twist, post, fwd, bwd,
        scratch=[
            pltpu.VMEM((COUNT, ROWS, height), jnp.float32),
            pltpu.VMEM((COUNT, ROWS, height), jnp.float32),
            pltpu.VMEM((2, 40, ROWS, LANE), jnp.float32),
            pltpu.VMEM((4 * SPAN, 2 * LANE), jnp.float32),
            pltpu.VMEM((4 * SPAN, 2 * LANE), jnp.float32),
        ],
        flops=3_000_000_000,
        vmem=24,
    )
    conv = exchange(conv_cols).reshape(width, height)
    response, energy = call(
        response_kernel,
        (block, jax.ShapeDtypeStruct((ROWS, height), jnp.float32)),
        query_t, conv,
    )
    others = [shifted(energy, "chan", k) for k in (2, 1, 3)]
    channels = width * lax.axis_size("chan")
    return call(
        functools.partial(norm_kernel, float(channels)),
        jax.ShapeDtypeStruct((height, width), jnp.float32),
        response, energy, *others,
        out_specs=HB,
        scratch=[
            pltpu.VMEM((height, width), jnp.float32),
            pltpu.SemaphoreType.DMA((height // LANE,)),
        ],
    )


def solution(mesh):
    return jax.shard_map(
        per_device,
        mesh=mesh,
        in_specs=(
            P("seq", "chan"),
            P("seq", "chan"),
            P("seq", "chan"),
            P("seq", "chan"),
            P(None, None, "chan"),
            P("chan"),
        ),
        out_specs=P("seq", "chan"),
        check_vma=False,
    )
```

```python
import functools
import math

import jax
import jax.numpy as jnp
import numpy as np
from jax import lax
from jax.experimental import pallas as pl
from jax.experimental.pallas import tpu as pltpu
from jax.sharding import PartitionSpec as P

LANE = 128
ROWS = 8


def dft8(values, sign):
    def add(a, b):
        if a is None:
            return b
        return a if b is None else a + b

    def sub(a, b):
        if b is None:
            return a
        return -b if a is None else a - b

    def cadd(x, y):
        return (add(x[0], y[0]), add(x[1], y[1]))

    def csub(x, y):
        return (sub(x[0], y[0]), sub(x[1], y[1]))

    def turn(x):
        re, im = x
        if sign > 0:
            return (None if im is None else -im, re)
        return (im, None if re is None else -re)

    def dft4(x):
        a, b = cadd(x[0], x[2]), csub(x[0], x[2])
        c, d = cadd(x[1], x[3]), turn(csub(x[1], x[3]))
        return [cadd(a, c), cadd(b, d), csub(a, c), csub(b, d)]

    even = dft4(values[0::2])
    odd = dft4(values[1::2])
    half = math.sqrt(0.5)
    out = [None] * 8
    for k in range(4):
        re, im = odd[k]
        if k == 0:
            turned = (re, im)
        elif k == 2:
            turned = turn((re, im))
        else:
            first = 1 if k == 1 else -1
            if im is None:
                turned = (first * half * re, sign * half * re)
            else:
                r = re if first > 0 else -re
                i = im if first > 0 else -im
                if sign > 0:
                    turned = (half * (r - im), half * (re + i))
                else:
                    turned = (half * (r + im), half * (i - re))
        out[k] = cadd(even[k], turned)
        out[k + 4] = csub(even[k], turned)
    return out


def cmul(x, y):
    return (x[0] * y[0] - x[1] * y[1], x[0] * y[1] + x[1] * y[0])


CLASSES = (
    [8 * v for v in range(5)]
    + [u + 8 * v for u in (1, 2, 3) for v in range(8)]
    + [4 + 8 * v for v in range(4)]
)
COUNT = len(CLASSES)
SPAN = COUNT * ROWS


def place(k):
    return CLASSES.index(k)


def tables(shards, width):
    total = shards * width
    where = np.arange(width)
    turns = (np.array(CLASSES)[:, None] * where[None, :]) % total
    angle = 2.0 * np.pi * turns / total
    twist = np.stack([np.cos(angle), np.sin(angle)]).astype(np.float32)
    quarter = width // 4
    inner = 2.0 * np.pi * np.arange(4)[:, None] * np.arange(quarter)[None, :] / width
    post = np.stack([np.cos(inner), np.sin(inner)]).astype(np.float32)
    turns = (np.arange(quarter)[:, None] * np.arange(quarter)[None, :]) % quarter
    angle = 2.0 * np.pi * turns / quarter
    c, s = np.cos(angle), np.sin(angle)
    forward = np.block([[c, -s], [s, c]])
    backward = np.block([[c, s], [-s, c]])

    def split(table):
        high = table.astype(np.float32).astype(jnp.bfloat16)
        low = (table - high.astype(np.float64)).astype(np.float32).astype(jnp.bfloat16)
        return np.concatenate([high, high, low])

    return twist[:, :, None, :], post[:, :, None, :], split(forward), split(backward)


def split_dot(values, table_ref):
    high = values.astype(jnp.bfloat16)
    low = (values - high.astype(jnp.float32)).astype(jnp.bfloat16)
    parts = jnp.concatenate([high, low, high], axis=1)
    return jnp.dot(parts, table_ref[...], preferred_element_type=jnp.float32)


UNROLL = 33


def over_classes(body):
    @pl.loop(0, COUNT // UNROLL)
    def _(i):
        for j in range(UNROLL):
            body(i * UNROLL + j)


def sections_forward(x_ref, at, mid_re, mid_im, stage, lane):
    sl = slice(lane * LANE, (lane + 1) * LANE)
    for b in range(8):
        col = [(x_ref[8 * a + b, at : at + ROWS, sl], None) for a in range(8)]
        out = dft8(col, -1)
        for u in range(5):
            re, im = out[u]
            if u and b:
                w = (math.cos(2 * math.pi * b * u / 64), -math.sin(2 * math.pi * b * u / 64))
                if im is None:
                    re, im = re * w[0], re * w[1]
                else:
                    re, im = cmul((re, im), w)
            stage[0, u * 8 + b] = re
            if im is not None:
                stage[1, u * 8 + b] = im
    for u in range(5):
        values = []
        for b in range(8):
            real_only = u == 0 or (u == 4 and b == 0)
            values.append(
                (stage[0, u * 8 + b], None if real_only else stage[1, u * 8 + b])
            )
        out = dft8(values, -1)
        for v in range(8):
            if u + 8 * v in CLASSES:
                k = place(u + 8 * v)
                re, im = out[v]
                mid_re[k, :, sl] = re
                mid_im[k, :, sl] = jnp.zeros_like(re) if im is None else im


def quarters_forward(mid_re, mid_im, twist, post, spec):
    @over_classes
    def _(at):
        z = []
        for h in range(4):
            sl = slice(h * LANE, (h + 1) * LANE)
            re, im = mid_re[at, :, sl], mid_im[at, :, sl]
            c, s = twist[0, at, :, sl], twist[1, at, :, sl]
            z.append((re * c + im * s, im * c - re * s))
        a = (z[0][0] + z[2][0], z[0][1] + z[2][1])
        b = (z[0][0] - z[2][0], z[0][1] - z[2][1])
        c = (z[1][0] + z[3][0], z[1][1] + z[3][1])
        d = (z[1][1] - z[3][1], z[3][0] - z[1][0])
        outs = [
            (a[0] + c[0], a[1] + c[1]),
            (b[0] + d[0], b[1] + d[1]),
            (a[0] - c[0], a[1] - c[1]),
            (b[0] - d[0], b[1] - d[1]),
        ]
        for q in range(4):
            re, im = outs[q]
            if q:
                c, s = post[0, q], post[1, q]
                re, im = re * c + im * s, im * c - re * s
            rows = pl.ds(pl.multiple_of(q * SPAN + at * ROWS, ROWS), ROWS)
            spec[rows, 0:LANE] = re
            spec[rows, LANE : 2 * LANE] = im


def quarters_backward(spec, mid_re, mid_im, twist, post):
    @over_classes
    def _(at):
        z = []
        for q in range(4):
            rows = pl.ds(pl.multiple_of(q * SPAN + at * ROWS, ROWS), ROWS)
            re, im = spec[rows, 0:LANE], spec[rows, LANE : 2 * LANE]
            if q:
                c, s = post[0, q], post[1, q]
                re, im = re * c - im * s, im * c + re * s
            z.append((re, im))
        a = (z[0][0] + z[2][0], z[0][1] + z[2][1])
        b = (z[0][0] - z[2][0], z[0][1] - z[2][1])
        c = (z[1][0] + z[3][0], z[1][1] + z[3][1])
        d = (z[3][1] - z[1][1], z[1][0] - z[3][0])
        outs = [
            (a[0] + c[0], a[1] + c[1]),
            (b[0] + d[0], b[1] + d[1]),
            (a[0] - c[0], a[1] - c[1]),
            (b[0] - d[0], b[1] - d[1]),
        ]
        for h in range(4):
            sl = slice(h * LANE, (h + 1) * LANE)
            re, im = outs[h]
            c, s = twist[0, at, :, sl], twist[1, at, :, sl]
            mid_re[at, :, sl] = re * c - im * s
            mid_im[at, :, sl] = im * c + re * s


def sections_backward(mid_re, mid_im, y_ref, stage, scale, lane):
    sl = slice(lane * LANE, (lane + 1) * LANE)
    for u in range(5):
        values = []
        for v in range(8):
            k = u + 8 * v
            if k in CLASSES:
                at = place(k)
                if k in (0, 32):
                    values.append((mid_re[at, :, sl], None))
                else:
                    values.append((mid_re[at, :, sl], mid_im[at, :, sl]))
            elif u == 0:
                re, im = values[8 - v]
                values.append((re, -im))
            else:
                at = place(64 - k)
                values.append((mid_re[at, :, sl], -mid_im[at, :, sl]))
        out = dft8(values, 1)
        for b in range(8):
            re, im = out[b]
            w = (
                scale * math.cos(2 * math.pi * b * u / 64),
                scale * math.sin(2 * math.pi * b * u / 64),
            )
            if u == 0:
                stage[0, b] = re * w[0]
            elif u == 4:
                stage[0, 32 + b] = re * w[0] - im * w[1]
            else:
                if b == 0:
                    re, im = re * w[0], im * w[0]
                else:
                    re, im = cmul((re, im), w)
                stage[0, u * 8 + b] = re
                stage[1, u * 8 + b] = im
    for b in range(8):
        values = [(stage[0, b], None)]
        for u in (1, 2, 3):
            values.append((stage[0, u * 8 + b], stage[1, u * 8 + b]))
        values.append((stage[0, 32 + b], None))
        for u in (3, 2, 1):
            values.append((values[u][0], -values[u][1]))
        out = dft8(values, 1)
        for a in range(8):
            y_ref[8 * a + b, :, sl] = out[a][0]


def convolve_kernel(
    scale, cols, twist, post, fwd, bwd, y_ref, mid_re, mid_im, stage, filt, spec
):
    for part, into in ((0, filt), (1, spec)):
        for lane in range(4):
            sections_forward(cols, part * ROWS, mid_re, mid_im, stage, lane)
        quarters_forward(mid_re, mid_im, twist, post, into)
        if part == 0:
            filt[...] = split_dot(filt[...], fwd)
    x = split_dot(spec[...], fwd)
    f = filt[...]
    re, im = cmul((x[:, :LANE], x[:, LANE:]), (f[:, :LANE], f[:, LANE:]))
    spec[...] = split_dot(jnp.concatenate([re, im], axis=1), bwd)
    quarters_backward(spec, mid_re, mid_im, twist, post)
    for lane in range(4):
        sections_backward(mid_re, mid_im, y_ref, stage, scale, lane)


VM = pl.BlockSpec(memory_space=pltpu.VMEM)
HB = pl.BlockSpec(memory_space=pltpu.HBM)
MIB = 1024 * 1024


def store_columns(out_ref, c, p, at, tile):
    turned = tile.T
    for g in range(tile.shape[1] // ROWS):
        out_ref[c // ROWS + g, at : at + ROWS, p : p + LANE] = turned[g * ROWS : (g + 1) * ROWS]


def short_filter(x_ref, halo, taps, p, c):
    tile = x_ref[p : p + LANE, c : c + LANE]
    if p == 0:
        before = jnp.concatenate([halo, tile[: LANE - 2]], axis=0)
        one = jnp.concatenate([halo[1:2], tile[: LANE - 1]], axis=0)
    else:
        before = x_ref[p - 2 : p + LANE - 2, c : c + LANE]
        one = x_ref[p - 1 : p + LANE - 1, c : c + LANE]
    return taps[0] * tile + taps[1] * one + taps[2] * before


def small_kernel(query_ref, key_ref, value_ref, taps_ref, skip_ref, ends_ref, out_ref, box, taps, skip, sems):
    height = query_ref.shape[0]
    copies = [
        pltpu.make_async_copy(ref.at[pl.ds(height - ROWS, ROWS)], box.at[g], sems.at[g])
        for g, ref in enumerate((query_ref, key_ref, value_ref))
    ]
    copies.append(pltpu.make_async_copy(taps_ref, taps, sems.at[3]))
    copies.append(pltpu.make_async_copy(skip_ref, skip, sems.at[4]))
    for copy in copies:
        copy.start()
    for copy in copies:
        copy.wait()
    for g in range(3):
        ends_ref[2 * g : 2 * g + 2, :] = box[g, ROWS - 2 :, :]
        out_ref[3 * g : 3 * g + 3, :] = taps[g]
    out_ref[9:10, :] = skip[...]


def taps_of(small_ref, g, sl):
    return [small_ref[3 * i + g : 3 * i + g + 1, sl] for i in range(3)]


def columns_kernel(filter_ref, key_ref, value_ref, small_ref, out_ref):
    height, width = key_ref.shape
    first = jnp.where(lax.axis_index("seq") == 0, 1.0, 0.0)
    for c in range(0, width, LANE):
        sl = slice(c, c + LANE)
        for p in range(0, height, LANE):
            tile = filter_ref[p : p + LANE, sl]
            if p == 0:
                row = lax.broadcasted_iota(jnp.int32, tile.shape, 0)
                tile = tile + jnp.where(row == 0, small_ref[9:10, sl] * first, 0.0)
            store_columns(out_ref, c, p, 0, tile)
            if p:
                k = short_filter(key_ref, None, taps_of(small_ref, 1, sl), p, c)
                v = short_filter(value_ref, None, taps_of(small_ref, 2, sl), p, c)
                store_columns(out_ref, c, p, ROWS, k * v)


def edge_kernel(key_ref, value_ref, halo_ref, small_ref, cols_ref, out_ref):
    del cols_ref
    width = key_ref.shape[1]
    for c in range(0, width, LANE):
        sl = slice(c, c + LANE)
        k = short_filter(key_ref, halo_ref[2 : 4, sl], taps_of(small_ref, 1, sl), 0, c)
        v = short_filter(value_ref, halo_ref[4 : 6, sl], taps_of(small_ref, 2, sl), 0, c)
        store_columns(out_ref, c, 0, ROWS, k * v)


def query_kernel(query_ref, halo_ref, small_ref, out_ref):
    height, width = query_ref.shape
    for c in range(0, width, LANE):
        sl = slice(c, c + LANE)
        for p in range(0, height, LANE):
            q = short_filter(query_ref, halo_ref[0 : 2, sl], taps_of(small_ref, 0, sl), p, c)
            out_ref[sl, p : p + LANE] = q.T


def response_kernel(query_ref, conv_ref, response_ref, energy_ref):
    height, width = query_ref.shape
    total = jnp.zeros((ROWS, width), jnp.float32)
    for r in range(0, height, ROWS):
        value = query_ref[r : r + ROWS, :] * conv_ref[r : r + ROWS, :]
        response_ref[r : r + ROWS, :] = value
        total = total + value * value
    energy_ref[...] = jnp.sum(total, axis=0, keepdims=True)


def norm_kernel(channels, response_ref, energy_ref, e1, e2, e3, out_ref, box, sems):
    height, width = response_ref.shape
    mean = (energy_ref[...] + e1[...] + e2[...] + e3[...]) / channels
    gain = 1.0 / jnp.sqrt(mean + 1e-06)
    copies = []
    for i, p in enumerate(range(0, width, LANE)):
        for c in range(0, height, LANE):
            tile = response_ref[c : c + LANE, p : p + LANE] * gain[:, p : p + LANE]
            box[p : p + LANE, c : c + LANE] = tile.T
        rows = pl.ds(p, LANE)
        copies.append(pltpu.make_async_copy(box.at[rows], out_ref.at[rows], sems.at[i]))
        copies[-1].start()
    for copy in copies:
        copy.wait()


def call(kernel, outs, *args, ins=None, out_specs=None, scratch=(), aliases=None, grid=(),
         vmem=16, flops=10_000_000, moved=4_000_000):
    return pl.pallas_call(
        kernel,
        out_shape=outs,
        grid=grid,
        in_specs=ins or [VM] * len(args),
        out_specs=out_specs or jax.tree.map(lambda _: VM, outs),
        scratch_shapes=scratch,
        input_output_aliases=aliases or {},
        compiler_params=pltpu.CompilerParams(vmem_limit_bytes=vmem * MIB),
        cost_estimate=pl.CostEstimate(flops=flops, bytes_accessed=moved, transcendentals=0),
    )(*args)


def exchange(values):
    return lax.all_to_all(values, "seq", split_axis=0, concat_axis=0, tiled=True)


def shifted(value, axis, steps):
    count = lax.axis_size(axis)
    return lax.ppermute(value, axis, [(i, (i + steps) % count) for i in range(count)])


def per_device(proj_query, proj_key, proj_value, long_filter, short_weight, skip_gain):
    height, width = proj_query.shape
    shards = lax.axis_size("seq")
    twist, post, fwd, bwd = (jnp.asarray(t) for t in tables(shards, height))
    block = jax.ShapeDtypeStruct((width, height), jnp.float32)
    pair = jax.ShapeDtypeStruct((shards, 2 * ROWS, height), jnp.float32)
    cube = jax.ShapeDtypeStruct((shards, ROWS, height), jnp.float32)

    ends, small = call(
        small_kernel,
        (
            jax.ShapeDtypeStruct((6, width), jnp.float32),
            jax.ShapeDtypeStruct((10, width), jnp.float32),
        ),
        proj_query, proj_key, proj_value, short_weight, skip_gain[None, :],
        ins=[HB] * 5,
        scratch=[
            pltpu.VMEM((3, ROWS, width), jnp.float32),
            pltpu.VMEM((3, 3, width), jnp.float32),
            pltpu.VMEM((1, width), jnp.float32),
            pltpu.SemaphoreType.DMA((5,)),
        ],
        moved=100_000,
        vmem=60,
    )
    halo = shifted(ends, "seq", 1)
    cols = call(
        columns_kernel, pair, long_filter, proj_key, proj_value, small
    )
    cols = call(
        edge_kernel, pair, proj_key, proj_value, halo, small, cols,
        aliases={4: 0},
        moved=1_000_000,
    )
    cols = exchange(cols)
    query_t = call(query_kernel, block, proj_query, halo, small)

    conv_cols = call(
        functools.partial(convolve_kernel, 1.0 / (shards * height)),
        cube,
        cols, twist, post, fwd, bwd,
        scratch=[
            pltpu.VMEM((COUNT, ROWS, height), jnp.float32),
            pltpu.VMEM((COUNT, ROWS, height), jnp.float32),
            pltpu.VMEM((2, 40, ROWS, LANE), jnp.float32),
            pltpu.VMEM((4 * SPAN, 2 * LANE), jnp.float32),
            pltpu.VMEM((4 * SPAN, 2 * LANE), jnp.float32),
        ],
        flops=3_000_000_000,
        vmem=24,
    )
    conv = exchange(conv_cols).reshape(width, height)
    response, energy = call(
        response_kernel,
        (block, jax.ShapeDtypeStruct((1, height), jnp.float32)),
        query_t, conv,
    )
    others = [shifted(energy, "chan", k) for k in (2, 1, 3)]
    channels = width * lax.axis_size("chan")
    return call(
        functools.partial(norm_kernel, float(channels)),
        jax.ShapeDtypeStruct((height, width), jnp.float32),
        response, energy, *others,
        out_specs=HB,
        scratch=[
            pltpu.VMEM((height, width), jnp.float32),
            pltpu.SemaphoreType.DMA((height // LANE,)),
        ],
    )


def solution(mesh):
    return jax.shard_map(
        per_device,
        mesh=mesh,
        in_specs=(
            P("seq", "chan"),
            P("seq", "chan"),
            P("seq", "chan"),
            P("seq", "chan"),
            P(None, None, "chan"),
            P("chan"),
        ),
        out_specs=P("seq", "chan"),
        check_vma=False,
    )
```
